256 devices in a mesh: rows: 2 (over core), trans: 16 (over x, z_hi), gvec: 8 (over y, z_lo).
Axes of the slice: x: 4, y: 4, z: 8 (z_hi: 4, z_lo: 2; z = z_hi * 2 + z_lo), core: 2. Of those that a mesh axis runs over, the one named last changes fastest.
Arguments:
- pair_density: bfloat16 [2, 16384, 4096], P(None, 'trans', 'gvec'), may hold values from -0.75 to 0.75
- coulomb: float32 [4096], P('gvec'), may hold values from 0.1 to 10
- block_index: int32 [2], P('rows'), parts along dimension 0, may hold values from 0 to 15
Outputs:
- kernel_rows: bfloat16 [2, 2048, 16384], P(None, ('rows', 'gvec'), 'trans'), parts along dimension 1
- mirrored: bfloat16 [2, 16384, 2048], P(None, 'trans', 'rows'), parts along dimension 2
The draws below stay inside these ranges and needn't reach their ends.
There are 2 independent parts, one for each index of `rows`. The reference program is written for one: setup_inputs(seed, part) draws one part's arguments, and reference() takes and returns one part's arrays. A program takes and returns all parts, laid end to end along the dimension named above; an argument that names none is the same for every part. Nothing has to cross between parts.
All inputs are finite; a program needn't handle non-finite values.
Results may differ from the reference program's by a relative error of at most 0.017.
Values may be sent and summed in bfloat16 or wider, within the bound.
No kernel may reach another device: no remote copies, remote signals or barrier semaphores. Data moves between devices by JAX's collectives and lax.ppermute only.
A program may use at most 64 MiB of HBM per device.

```python
import math
import jax
import jax.numpy as jnp
from jax import lax

NG = 4096
TR_DEV = 1024
NT = 16384
N_TRANS = 16
N_GVEC = 8


def levels(stream_key, extent, split, low, high):
    def one(dim, blocks):
        heights = jax.random.uniform(jax.random.fold_in(jax.random.fold_in(stream_key, 6), dim), (blocks,), jnp.float32, low / len(split), high / len(split))
        return jnp.repeat(jnp.exp(heights), extent[dim] // blocks).reshape((-1,) + (1,) * (len(extent) - dim - 1))

    loudness = one(*split[0])
    for cut in split[1:]:
        loudness = loudness * one(*cut)
    return loudness


def gaussian(stream_key, extent, spread, bound, shards=(), held_as=jnp.bfloat16):
    drawn = spread * jax.random.normal(stream_key, extent, jnp.float32)
    if shards:
        drawn = drawn * levels(stream_key, extent, shards, -0.22, 0.18)
    return jnp.clip(drawn, -bound, bound).astype(held_as)


def setup_inputs(seed: int = 0, part: int = 0) -> dict:
    splits = jax.random.split(jax.random.key(seed), 4)
    own_keys = jax.random.split(jax.random.fold_in(splits[3], part), 4)
    pair_density = gaussian(splits[0], (2, NT, NG), (NG ** -0.25), 0.75, ((1, 16), (2, 8)))
    coulomb = jnp.clip(jnp.exp(math.log(10.0) - 4.6051702 * jax.random.uniform(splits[1], (NG,), jnp.float32) ** levels(splits[1], (NG,), ((0, 8),), -0.2, 0.2)), 0.1, 10.0)
    block_index = jax.random.randint(own_keys[2], (1,), 0, N_TRANS).astype(jnp.int32)
    return {"pair_density": pair_density, "coulomb": coulomb, "block_index": block_index}


def contract(left, right):
    return lax.dot_general(left, right, (((1,), (1,)), ((), ())), precision=lax.Precision.HIGHEST, preferred_element_type=jnp.float32)


def reference(pair_density, coulomb, block_index):
    start = (block_index[0] * TR_DEV).astype(jnp.int32)
    block = lax.dynamic_slice_in_dim(pair_density, start, TR_DEV, 1)
    weighted = (block.astype(jnp.float32) * coulomb[None, None, :]).astype(jnp.bfloat16)
    width = NG // N_GVEC
    real_part = jnp.zeros((TR_DEV, TR_DEV * N_TRANS), jnp.float32)
    imag_part = jnp.zeros((TR_DEV, TR_DEV * N_TRANS), jnp.float32)
    for group in range(N_GVEC):
        low = group * width
        left_real = weighted[0, :, low:low + width].astype(jnp.float32)
        left_imag = weighted[1, :, low:low + width].astype(jnp.float32)
        right_real = pair_density[0, :, low:low + width].astype(jnp.float32)
        right_imag = pair_density[1, :, low:low + width].astype(jnp.float32)
        term_real = (contract(left_real, right_real) + contract(left_imag, right_imag)).astype(jnp.bfloat16)
        term_imag = (contract(left_real, right_imag) - contract(left_imag, right_real)).astype(jnp.bfloat16)
        term_real, term_imag = lax.optimization_barrier((term_real, term_imag))
        real_part = real_part + term_real.astype(jnp.float32)
        imag_part = imag_part + term_imag.astype(jnp.float32)
    real_out = real_part.astype(jnp.bfloat16)
    imag_out = imag_part.astype(jnp.bfloat16)
    kernel_rows = jnp.stack([real_out, imag_out])
    mirrored = jnp.stack([real_out.T, -imag_out.T])
    return kernel_rows, mirrored
```

```python
import jax
import jax.numpy as jnp
from jax import lax
from jax.sharding import PartitionSpec as P

BF16 = jnp.bfloat16
F32 = jnp.float32


def along_x(step):
    return [(4 * x + z, 4 * ((x + step) % 4) + z) for x in range(4) for z in range(4)]


def along_z(step):
    return [(4 * x + z, 4 * x + (z + step) % 4) for x in range(4) for z in range(4)]


def along_y(step):
    return [(2 * y + p, 2 * ((y + step) % 4) + p) for y in range(4) for p in range(2)]


PAIR = [(2 * y + p, 2 * y + 1 - p) for y in range(4) for p in range(2)]
CORE = [(0, 1), (1, 0)]


def send(value, axis, pairs):
    return lax.ppermute(value, axis, pairs)


def pick(value, index, axis):
    return lax.dynamic_index_in_dim(value, index, axis, keepdims=False)


def put(buffer, value, index, axis):
    return lax.dynamic_update_index_in_dim(buffer, value, index, axis)


def choose(source, candidates):
    out = candidates[0]
    for d in range(1, 4):
        out = jnp.where(source == d, candidates[d], out)
    return out


def exchange(value, axis, place, name, pairs):
    got = [pick(value, place, axis)]
    for d in range(1, 4):
        got.append(send(pick(value, (place + d) % 4, axis), name, pairs(d)))
    return got


def ring_gather(value, name, pairs, cut):
    below = send(value, name, pairs(1))
    above = send(value, name, pairs(-1))
    half = value.shape[cut] // 2
    first = lax.slice_in_dim(below, 0, half, axis=cut)
    second = lax.slice_in_dim(above, half, 2 * half, axis=cut)
    across = lax.concatenate(
        [send(first, name, pairs(1)), send(second, name, pairs(-1))], cut
    )
    return [value, below, across, above]


def contract(left, right):
    return lax.dot_general(
        left, right, (((1,), (1,)), ((), ())), preferred_element_type=F32
    )


def body(pair_density, coulomb, block_index):
    core = lax.axis_index("rows")
    trans = lax.axis_index("trans")
    gvec = lax.axis_index("gvec")
    x, z = trans // 4, trans % 4
    y, p = gvec // 2, gvec % 2
    block = block_index[0]
    other_block = send(block_index, "rows", CORE)[0]

    mine = pick(pair_density, core, 0)
    parts = mine.reshape(4, 2, 4, 4, 8, 512)
    got = exchange(parts, 2, x, "trans", along_x)
    own = choose((x - block // 4) % 4, got)
    swapped = send(choose((x - other_block // 4) % 4, got), "rows", CORE)
    share = jnp.where(core == 0, jnp.stack([own, swapped]), jnp.stack([swapped, own]))

    got = exchange(share, 3, z, "trans", along_z)
    share = choose((z - block % 4) % 4, got)
    share = (share.astype(F32) * coulomb).astype(BF16)
    share = jnp.concatenate(exchange(share, 1, y, "gvec", along_y), axis=3)

    weighted = jnp.zeros((2, 2, 4, 8, 2048), BF16)
    for d, value in enumerate(ring_gather(share, "trans", along_z, 1)):
        weighted = put(weighted, value, (z - d) % 4, 2)
    whole = jnp.zeros((2, 2, 4, 4, 8, 2048), BF16)
    for d, value in enumerate(ring_gather(weighted, "trans", along_x, 1)):
        whole = put(whole, value, (x - d) % 4, 2)
    whole = whole.reshape(2, 256, 2048)

    gathered = jnp.concatenate(ring_gather(mine, "gvec", along_y, 0)[0:], axis=1)
    twin = send(gathered[:, 512:], "rows", CORE)
    twin = jnp.concatenate([pick(pair_density, 1 - core, 0), twin], axis=1)
    right = jnp.where(core == 0, jnp.stack([gathered, twin]), jnp.stack([twin, gathered]))

    real_part = contract(whole[0], right[0]) + contract(whole[1], right[1])
    imag_part = contract(whole[0], right[1]) - contract(whole[1], right[0])
    partial_terms = jnp.stack([real_part, imag_part]).astype(BF16).reshape(2, 2, 128, 1024)
    coming = send(pick(partial_terms, 1 - p, 1), "gvec", PAIR)
    kernel_rows = (pick(partial_terms, p, 1).astype(F32) + coming.astype(F32)).astype(BF16)

    partner = send(kernel_rows, "gvec", PAIR)
    pair = jnp.where(
        p == 0, jnp.stack([kernel_rows, partner], 1), jnp.stack([partner, kernel_rows], 1)
    ).reshape(2, 256, 1024)
    full = jnp.zeros((2, 4, 256, 1024), BF16)
    for d, value in enumerate(ring_gather(pair, "gvec", along_y, 1)):
        full = put(full, value, (y - d) % 4, 1)
    full = full.reshape(2, 1024, 1024)
    mirrored = jnp.stack([full[0].T, -full[1].T])
    return (kernel_rows, mirrored)


def solution(mesh):
    placed = (P(None, "trans", "gvec"), P("gvec"), P("rows"))
    return jax.shard_map(
        body,
        mesh=mesh,
        in_specs=placed,
        out_specs=(P(None, ("rows", "gvec"), "trans"), P(None, "trans", "rows")),
        check_vma=False,
    )
```

```python
import functools

import jax
import jax.numpy as jnp
from jax import lax
from jax.experimental import pallas as pl
from jax.experimental.pallas import tpu as pltpu
from jax.sharding import PartitionSpec as P

BF16 = jnp.bfloat16
F32 = jnp.float32
X_GROUPS = [[4 * x + z for x in range(4)] for z in range(4)]
ZY_GROUPS = [
    [8 * (4 * x + z) + 2 * y + p for z in range(4) for y in range(4)]
    for x in range(4)
    for p in range(2)
]
PAIR = [(2 * y + p, 2 * y + 1 - p) for y in range(4) for p in range(2)]
CORE = [(0, 1), (1, 0)]
LIMIT = 48 * 1024 * 1024


def along_x(step):
    return [(4 * x + z, 4 * ((x + step) % 4) + z) for x in range(4) for z in range(4)]


def along_z(step):
    return [(4 * x + z, 4 * x + (z + step) % 4) for x in range(4) for z in range(4)]


def along_y(step):
    return [(2 * y + p, 2 * ((y + step) % 4) + p) for y in range(4) for p in range(2)]


def send(value, axis, pairs):
    return lax.ppermute(value, axis, pairs)


def pick(value, index, axis):
    return lax.dynamic_index_in_dim(value, index, axis, keepdims=False)


def from_below(value, axis, pairs):
    one, three = send(value, axis, pairs(1)), send(value, axis, pairs(3))
    return one, send(value, axis, pairs(2)), three


def multiply_kernel(count, place_ref, *refs):
    chunks, right, out_ref = refs[:count], refs[count:-1], refs[-1]
    y, sign = place_ref[0], place_ref[1].astype(F32)
    for i, chunk_ref in enumerate(chunks):
        sums = []
        for component in range(2):
            total = None
            for d in range(4):
                left = chunk_ref[lax.rem(y + 4 - d, 4)].reshape(128, 512)
                term = lax.dot_general(
                    left,
                    right[4 * component + d][...],
                    (((1,), (1,)), ((), ())),
                    preferred_element_type=F32,
                )
                total = term if total is None else total + term
            sums.append(total)
        mine, twin = sums
        rows = pl.ds(64 * i, 64)
        out_ref[0, rows, :] = (mine[:64] + twin[64:]).astype(BF16)
        out_ref[1, rows, :] = (sign * (twin[:64] - mine[64:])).astype(BF16)


def multiply(place, chunks, right):
    count = len(chunks)
    return pl.pallas_call(
        functools.partial(multiply_kernel, count),
        grid_spec=pltpu.PrefetchScalarGridSpec(
            num_scalar_prefetch=1,
            grid=(4,),
            in_specs=[pl.BlockSpec((4, 2, 64, 512), lambda t, s: (0, 0, 0, 0))] * count
            + [pl.BlockSpec((256, 512), lambda t, s: (t, 0))] * 8,
            out_specs=pl.BlockSpec((2, 64 * count, 256), lambda t, s: (0, 0, t)),
        ),
        out_shape=jax.ShapeDtypeStruct((2, 64 * count, 1024), BF16),
        compiler_params=pltpu.CompilerParams(vmem_limit_bytes=LIMIT),
        cost_estimate=pl.CostEstimate(
            flops=count * 2**30, bytes_accessed=9 * 2**20, transcendentals=0
        ),
    )(place, *chunks, *right)


def place_rows(ref, start, value_ref, first, z):
    for k in range(4):
        to = pl.multiple_of(start + 16 * lax.rem(z + 4 - k, 4), 16)
        ref[pl.ds(to, 16), :] = value_ref[0, pl.ds(first + 16 * k, 16), :]


def place_chunks(ref, refs, x, z):
    own, sides, across = refs
    place_rows(ref, 64 * x, own, 0, z)
    place_rows(ref, 64 * lax.rem(x + 3, 4), sides, 0, z)
    place_rows(ref, 64 * lax.rem(x + 1, 4), sides, 64, z)
    place_rows(ref, 64 * lax.rem(x + 2, 4), across, 0, z)


def mirror_kernel(place_ref, *refs):
    pieces, out_ref, scratch = refs[:12], refs[12], refs[13]
    y, x, z = place_ref[0], place_ref[2], place_ref[3]
    sign = jnp.where(pl.program_id(0) == 0, 1.0, -1.0).astype(F32)
    for d in range(4):
        held = scratch.at[d]
        place_chunks(held, pieces[3 * d : 3 * d + 3], x, z)
        columns = pl.ds(pl.multiple_of(256 * lax.rem(y + 4 - d, 4), 256), 256)
        out_ref[0, :, columns] = (held[...].astype(F32) * sign).T.astype(BF16)


def piece_specs(width):
    return [
        pl.BlockSpec((1, rows, width), lambda c, t, s: (c, 0, t)) for rows in (64, 128, 64)
    ]


def mirror(place, pieces):
    return pl.pallas_call(
        mirror_kernel,
        grid_spec=pltpu.PrefetchScalarGridSpec(
            num_scalar_prefetch=1,
            grid=(2, 4),
            in_specs=piece_specs(256) * 4,
            out_specs=pl.BlockSpec((1, 256, 1024), lambda c, t, s: (c, t, 0)),
            scratch_shapes=[pltpu.VMEM((4, 256, 256), BF16)],
        ),
        out_shape=jax.ShapeDtypeStruct((2, 1024, 1024), BF16),
        compiler_params=pltpu.CompilerParams(vmem_limit_bytes=LIMIT),
        cost_estimate=pl.CostEstimate(flops=0, bytes_accessed=8 * 2**20, transcendentals=0),
    )(place, *pieces)


def rows_kernel(place_ref, own, sides, across, out_ref, scratch):
    x, z, p = place_ref[2], place_ref[3], place_ref[4]
    place_chunks(scratch, (own, sides, across), x, z)
    out_ref[0] = scratch[pl.ds(pl.multiple_of(128 * p, 128), 128), :]


def own_rows(place, pieces):
    return pl.pallas_call(
        rows_kernel,
        grid_spec=pltpu.PrefetchScalarGridSpec(
            num_scalar_prefetch=1,
            grid=(2, 1),
            in_specs=piece_specs(1024),
            out_specs=pl.BlockSpec((1, 128, 1024), lambda c, t, s: (c, 0, t)),
            scratch_shapes=[pltpu.VMEM((256, 1024), BF16)],
        ),
        out_shape=jax.ShapeDtypeStruct((2, 128, 1024), BF16),
        compiler_params=pltpu.CompilerParams(vmem_limit_bytes=LIMIT),
        cost_estimate=pl.CostEstimate(flops=0, bytes_accessed=3 * 2**19, transcendentals=0),
    )(place, *pieces)


def body(pair_density, coulomb, block_index):
    core = lax.axis_index("rows")
    trans = lax.axis_index("trans")
    gvec = lax.axis_index("gvec")
    x, z = trans // 4, trans % 4
    y, p = gvec // 2, gvec % 2
    place = jnp.stack([y, 1 - 2 * core, x, z, p]).astype(jnp.int32)
    block = block_index[0]
    other_block = send(block_index, "rows", CORE)[0]

    mine = pick(pair_density, core, 0)
    gathered = from_below(mine, "gvec", along_y)
    twin = pick(pair_density, 1 - core, 0)
    right = [mine, *gathered, twin, *(send(value, "rows", CORE) for value in gathered)]

    parts = mine.reshape(4, 4, 64, 512).transpose(1, 0, 2, 3)
    got = lax.all_to_all(parts, "trans", 0, 0, axis_index_groups=X_GROUPS, tiled=True)
    swapped = send(pick(got, other_block // 4, 0), "rows", CORE)
    share = jnp.stack([pick(got, block // 4, 0), swapped], axis=1)
    share = (share.astype(F32) * coulomb).astype(BF16)
    share = share.reshape(4, 2, 4, 16, 512).transpose(2, 0, 1, 3, 4).reshape(16, 2, 16, 512)
    got = lax.all_to_all(
        share, ("trans", "gvec"), 0, 0, axis_index_groups=ZY_GROUPS, tiled=True
    )
    share = pick(got.reshape(4, 4, 2, 16, 512), block % 4, 0)
    chunk = jnp.concatenate([share, *from_below(share, "trans", along_z)], axis=2)
    below, across, above = from_below(chunk, "trans", along_x)

    pieces = []
    for chunks in ((chunk,), (below, above), (across,)):
        partial_terms = multiply(place, chunks, right)
        coming = send(partial_terms, "gvec", PAIR)
        summed = (partial_terms.astype(F32) + coming.astype(F32)).astype(BF16)
        pieces.append((summed, *from_below(summed, "gvec", along_y)))
    kernel_rows = own_rows(place, [piece[0] for piece in pieces])
    mirrored = mirror(place, [piece[d] for d in range(4) for piece in pieces])
    return (kernel_rows, mirrored)


def solution(mesh):
    placed = (P(None, "trans", "gvec"), P("gvec"), P("rows"))
    return jax.shard_map(
        body,
        mesh=mesh,
        in_specs=placed,
        out_specs=(P(None, ("rows", "gvec"), "trans"), P(None, "trans", "rows")),
        check_vma=False,
    )
```

```python
import jax
import jax.numpy as jnp
from jax import lax
from jax.experimental import pallas as pl
from jax.experimental.pallas import tpu as pltpu
from jax.sharding import PartitionSpec as P

BF16 = jnp.bfloat16
F32 = jnp.float32
PAIR = [(2 * y + p, 2 * y + 1 - p) for y in range(4) for p in range(2)]
CORE = [(0, 1), (1, 0)]
LIMIT = 24 * 1024 * 1024


def along_x(step):
    return [(4 * x + z, 4 * ((x + step) % 4) + z) for x in range(4) for z in range(4)]


def along_z(step):
    return [(4 * x + z, 4 * x + (z + step) % 4) for x in range(4) for z in range(4)]


def along_y(step):
    return [(2 * y + p, 2 * ((y + step) % 4) + p) for y in range(4) for p in range(2)]


def send(value, axis, pairs):
    return lax.ppermute(value, axis, pairs)


def pick(value, index, axis):
    return lax.dynamic_index_in_dim(value, index, axis, keepdims=False)


def choose(distance, candidates):
    out = candidates[0]
    for d in range(1, 4):
        out = jnp.where(distance == d, candidates[d], out)
    return out


def from_below(value, axis, pairs):
    one, three = send(value, axis, pairs(1)), send(value, axis, pairs(3))
    return one, send(value, axis, pairs(2)), three


def tie(value, *others):
    return lax.optimization_barrier((value, *others))[0]


def multiply(chunk, sign, right):
    rows, half = chunk.shape[0], chunk.shape[1] // 2
    turned = jnp.concatenate([-chunk[:, half:], chunk[:, :half]], axis=1) * sign
    left = jnp.concatenate([chunk, turned], axis=0)
    return contract(left, right).astype(BF16).reshape(2, rows, right.shape[0])


def contract(left, right):
    return lax.dot_general(
        left, right, (((1,), (1,)), ((), ())), preferred_element_type=F32
    )


def place_rows(ref, start, value, z):
    for k in range(4):
        to = pl.multiple_of(start + 16 * lax.rem(z + 4 - k, 4), 16)
        ref[pl.ds(to, 16), :] = value[16 * k : 16 * k + 16]


def place_others(ref, value, x, z):
    for d in range(1, 4):
        place_rows(ref, 64 * lax.rem(x + 4 - d, 4), value[64 * d - 64 : 64 * d], z)


def mirror_kernel(place_ref, *refs):
    scratch, out_ref = refs[-1], refs[-2]
    y, x, z = place_ref[0], place_ref[1], place_ref[2]
    sign = jnp.where(pl.program_id(0) == 0, 1.0, -1.0).astype(BF16)
    for d in range(4):
        held = scratch.at[d]
        place_rows(held, 64 * x, refs[2 * d][0], z)
        place_others(held, refs[2 * d + 1][0], x, z)
        columns = pl.ds(pl.multiple_of(256 * lax.rem(y + 4 - d, 4), 256), 256)
        out_ref[0, :, columns] = held[...].T * sign


def mirror(place, held, half, pieces):
    specs = [
        pl.BlockSpec((1, 64, 256), lambda c, t, s: (c, 0, 2 * half + t)),
        pl.BlockSpec((1, 192, 256), lambda c, t, s: (c, 0, t)),
    ] * 4
    operands, aliases = list(pieces), {}
    if held is not None:
        specs.append(pl.BlockSpec(memory_space=pl.ANY))
        operands.append(held)
        aliases = {len(operands): 0}
    return pl.pallas_call(
        mirror_kernel,
        grid_spec=pltpu.PrefetchScalarGridSpec(
            num_scalar_prefetch=1,
            grid=(2, 2),
            in_specs=specs,
            out_specs=pl.BlockSpec((1, 256, 1024), lambda c, t, s: (c, 2 * half + t, 0)),
            scratch_shapes=[pltpu.VMEM((4, 256, 256), BF16)],
        ),
        out_shape=jax.ShapeDtypeStruct((2, 1024, 1024), BF16),
        input_output_aliases=aliases,
        compiler_params=pltpu.CompilerParams(vmem_limit_bytes=LIMIT),
        cost_estimate=pl.CostEstimate(flops=0, bytes_accessed=2**22, transcendentals=0),
    )(place, *operands)


def rows_kernel(place_ref, own, low, high, out_ref, scratch):
    x, z, p = place_ref[1], place_ref[2], place_ref[3]
    place_rows(scratch, 64 * x, own[0], z)
    for half, value in enumerate((low, high)):
        place_others(scratch.at[:, pl.ds(512 * half, 512)], value[0], x, z)
    out_ref[0] = scratch[pl.ds(pl.multiple_of(128 * p, 128), 128), :]


def own_rows(place, pieces):
    return pl.pallas_call(
        rows_kernel,
        grid_spec=pltpu.PrefetchScalarGridSpec(
            num_scalar_prefetch=1,
            grid=(2,),
            in_specs=[
                pl.BlockSpec((1, *piece.shape[1:]), lambda c, s: (c, 0, 0)) for piece in pieces
            ],
            out_specs=pl.BlockSpec((1, 128, 1024), lambda c, s: (c, 0, 0)),
            scratch_shapes=[pltpu.VMEM((256, 1024), BF16)],
        ),
        out_shape=jax.ShapeDtypeStruct((2, 128, 1024), BF16),
        compiler_params=pltpu.CompilerParams(vmem_limit_bytes=LIMIT),
        cost_estimate=pl.CostEstimate(flops=0, bytes_accessed=3 * 2**19, transcendentals=0),
    )(place, *pieces)


def body(pair_density, coulomb, block_index):
    core = lax.axis_index("rows")
    trans = lax.axis_index("trans")
    gvec = lax.axis_index("gvec")
    x, z = trans // 4, trans % 4
    y, p = gvec // 2, gvec % 2
    place = jnp.stack([y, x, z, p]).astype(jnp.int32)
    block = block_index[0]
    other_block = send(block_index, "rows", CORE)[0]

    mine = pick(pair_density, core, 0)
    twin = pick(pair_density, 1 - core, 0)
    below = send(mine, "gvec", along_y(1))
    above = send(mine, "gvec", along_y(3))

    parts = mine.reshape(4, 4, 64, 512)
    got = [pick(parts, x, 1)]
    got += [send(pick(parts, (x + d) % 4, 1), "trans", along_x(d)) for d in (1, 2, 3)]
    swapped = send(choose((x - other_block // 4) % 4, got), "rows", CORE)
    share = jnp.stack([choose((x - block // 4) % 4, got), swapped], axis=1)
    share = (share.astype(F32) * coulomb).astype(BF16)
    share = share.reshape(4, 2, 4, 16, 512)
    got = [pick(share, z, 2)]
    got += [send(pick(share, (z + d) % 4, 2), "trans", along_z(d)) for d in (1, 2, 3)]
    share = choose((z - block % 4) % 4, got)
    low = send(below[:512], "gvec", along_y(1))
    high = send(above[512:], "gvec", along_y(3))
    share = tie(share, low, high)
    below_twin = send(below, "rows", CORE)
    above_twin = send(above, "rows", CORE)
    got = [pick(share, y, 0)]
    got += [send(pick(share, (y + d) % 4, 0), "gvec", along_y(d)) for d in (1, 2, 3)]
    share = jnp.concatenate([piece[c] for c in range(2) for piece in got], axis=1)
    share = tie(share, below_twin, above_twin)
    low_twin = send(low, "rows", CORE)
    high_twin = send(high, "rows", CORE)
    first = [mine, below, None, above, twin, below_twin, None, above_twin]
    right = []
    for half, pair in enumerate(((low, low_twin), (high, high_twin))):
        parts = [v if v is None else v[512 * half : 512 * half + 512] for v in first]
        parts[2], parts[6] = pair
        right.append(jnp.concatenate(parts, axis=1))
    chunk = jnp.concatenate([share, *from_below(share, "trans", along_z)], axis=0)
    chunk, right = lax.optimization_barrier((chunk, right))
    others = from_below(chunk, "trans", along_x)
    sign = (1 - 2 * core).astype(BF16)

    def add(one, other):
        return (one.astype(F32) + other.astype(F32)).astype(BF16)

    own_terms = jnp.concatenate([multiply(chunk, sign, half) for half in right], axis=2)
    own_sum = add(own_terms, send(own_terms, "gvec", PAIR))
    own_piece = (own_sum, *from_below(own_sum, "gvec", along_y))
    others = tie(jnp.concatenate(others), own_sum)
    low_terms = multiply(others, sign, right[0])
    high_terms = multiply(tie(others, low_terms), sign, right[1])
    low_sum = add(low_terms, send(low_terms, "gvec", PAIR))
    low_sum = tie(low_sum, high_terms, *own_piece)
    low_piece = (low_sum, *from_below(low_sum, "gvec", along_y))
    high_sum = add(high_terms, send(high_terms, "gvec", PAIR))
    high_piece = (high_sum, *from_below(high_sum, "gvec", along_y))
    kernel_rows = own_rows(place, (own_sum, low_sum, high_sum))
    mirrored = None
    for half, piece in enumerate((low_piece, high_piece)):
        pieces = [value for d in range(4) for value in (own_piece[d], piece[d])]
        mirrored = mirror(place, mirrored, half, pieces)
    return (kernel_rows, mirrored)


def solution(mesh):
    placed = (P(None, "trans", "gvec"), P("gvec"), P("rows"))
    return jax.shard_map(
        body,
        mesh=mesh,
        in_specs=placed,
        out_specs=(P(None, ("rows", "gvec"), "trans"), P(None, "trans", "rows")),
        check_vma=False,
    )
```

```python
import jax
import jax.numpy as jnp
from jax import lax
from jax.experimental import pallas as pl
from jax.experimental.pallas import tpu as pltpu
from jax.sharding import PartitionSpec as P

BF16 = jnp.bfloat16
F32 = jnp.float32
PAIR = [(2 * y + p, 2 * y + 1 - p) for y in range(4) for p in range(2)]
CORE = [(0, 1), (1, 0)]
LIMIT = 24 * 1024 * 1024


def along_x(step):
    return [(4 * x + z, 4 * ((x + step) % 4) + z) for x in range(4) for z in range(4)]


def along_z(step):
    return [(4 * x + z, 4 * x + (z + step) % 4) for x in range(4) for z in range(4)]


def along_y(step):
    return [(2 * y + p, 2 * ((y + step) % 4) + p) for y in range(4) for p in range(2)]


def send(value, axis, pairs):
    return lax.ppermute(value, axis, pairs)


def pick(value, index, axis):
    return lax.dynamic_index_in_dim(value, index, axis, keepdims=False)


def gather(value):
    one, three = send(value, "gvec", along_y(1)), send(value, "gvec", along_y(3))
    two = send(one[0], "gvec", along_y(1)), send(three[1], "gvec", along_y(3))
    return value, one, two, three


def choose(distance, candidates):
    out = candidates[0]
    for d in range(1, 4):
        out = jnp.where(distance == d, candidates[d], out)
    return out


def from_below(value, axis, pairs):
    one, three = send(value, axis, pairs(1)), send(value, axis, pairs(3))
    return one, send(value, axis, pairs(2)), three


def tie(value, *others):
    return lax.optimization_barrier((value, *others))[0]


def multiply(chunk, sign, right):
    rows, half = chunk.shape[0], chunk.shape[1] // 2
    turned = jnp.concatenate([-chunk[:, half:], chunk[:, :half]], axis=1) * sign
    left = jnp.concatenate([chunk, turned], axis=0)
    return contract(left, right).astype(BF16).reshape(2, rows, right.shape[0])


def contract(left, right):
    return lax.dot_general(
        left, right, (((1,), (1,)), ((), ())), preferred_element_type=F32
    )


def place_rows(ref, start, value, z, first=0):
    for k in range(4):
        to = pl.multiple_of(start + 16 * lax.rem(z + 4 - k, 4), 16)
        ref[pl.ds(to, 16), :] = value[first + 16 * k : first + 16 * k + 16, :]


def place_others(ref, value, x, z):
    for d in range(1, 4):
        place_rows(ref, 64 * lax.rem(x + 4 - d, 4), value, z, 64 * d - 64)


def mirror_kernel(place_ref, *refs):
    scratch, out_ref = refs[-1], refs[-2]
    y, x, z = place_ref[0], place_ref[1], place_ref[2]
    sign = jnp.where(pl.program_id(0) == 0, 1.0, -1.0).astype(BF16)
    groups = [refs[0:2], refs[2:4], None, refs[8:10]]
    for d in range(4):
        held = scratch.at[d]
        if d == 2:
            first = pl.program_id(0) == 0
            own = jnp.where(first, refs[4][...], refs[6][...])
            others = jnp.where(first, refs[5][...], refs[7][...])
        else:
            own, others = groups[d][0].at[0], groups[d][1].at[0]
        place_rows(held, 64 * x, own, z)
        place_others(held, others, x, z)
        columns = pl.ds(pl.multiple_of(256 * lax.rem(y + 4 - d, 4), 256), 256)
        out_ref[0, :, columns] = held[...].T * sign


def mirror(place, held, half, pieces):
    whole = [
        pl.BlockSpec((1, 64, 256), lambda c, t, s: (c, 0, 2 * half + t)),
        pl.BlockSpec((1, 192, 256), lambda c, t, s: (c, 0, t)),
    ]
    single = [
        pl.BlockSpec((64, 256), lambda c, t, s: (0, 2 * half + t)),
        pl.BlockSpec((192, 256), lambda c, t, s: (0, t)),
    ]
    specs = [*whole * 2, *single * 2, *whole]
    operands, aliases = list(pieces), {}
    if held is not None:
        specs.append(pl.BlockSpec(memory_space=pl.ANY))
        operands.append(held)
        aliases = {len(operands): 0}
    return pl.pallas_call(
        mirror_kernel,
        grid_spec=pltpu.PrefetchScalarGridSpec(
            num_scalar_prefetch=1,
            grid=(2, 2),
            in_specs=specs,
            out_specs=pl.BlockSpec((1, 256, 1024), lambda c, t, s: (c, 2 * half + t, 0)),
            scratch_shapes=[pltpu.VMEM((4, 256, 256), BF16)],
        ),
        out_shape=jax.ShapeDtypeStruct((2, 1024, 1024), BF16),
        input_output_aliases=aliases,
        compiler_params=pltpu.CompilerParams(vmem_limit_bytes=LIMIT),
        cost_estimate=pl.CostEstimate(flops=0, bytes_accessed=2**22, transcendentals=0),
    )(place, *operands)


def rows_kernel(place_ref, own, low, high, out_ref, scratch):
    x, z, p = place_ref[1], place_ref[2], place_ref[3]
    place_rows(scratch, 64 * x, own.at[0], z)
    for half, value in enumerate((low, high)):
        place_others(scratch.at[:, pl.ds(512 * half, 512)], value.at[0], x, z)
    out_ref[0] = scratch[pl.ds(pl.multiple_of(128 * p, 128), 128), :]


def own_rows(place, pieces):
    return pl.pallas_call(
        rows_kernel,
        grid_spec=pltpu.PrefetchScalarGridSpec(
            num_scalar_prefetch=1,
            grid=(2,),
            in_specs=[
                pl.BlockSpec((1, *piece.shape[1:]), lambda c, s: (c, 0, 0)) for piece in pieces
            ],
            out_specs=pl.BlockSpec((1, 128, 1024), lambda c, s: (c, 0, 0)),
            scratch_shapes=[pltpu.VMEM((256, 1024), BF16)],
        ),
        out_shape=jax.ShapeDtypeStruct((2, 128, 1024), BF16),
        compiler_params=pltpu.CompilerParams(vmem_limit_bytes=LIMIT),
        cost_estimate=pl.CostEstimate(flops=0, bytes_accessed=3 * 2**19, transcendentals=0),
    )(place, *pieces)


def body(pair_density, coulomb, block_index):
    core = lax.axis_index("rows")
    trans = lax.axis_index("trans")
    gvec = lax.axis_index("gvec")
    x, z = trans // 4, trans % 4
    y, p = gvec // 2, gvec % 2
    place = jnp.stack([y, x, z, p]).astype(jnp.int32)
    block = block_index[0]
    other_block = send(block_index, "rows", CORE)[0]

    mine = pick(pair_density, core, 0)
    twin = pick(pair_density, 1 - core, 0)
    below = send(mine, "gvec", along_y(1))
    above = send(mine, "gvec", along_y(3))

    parts = mine.reshape(4, 4, 64, 512)
    got = [pick(parts, x, 1)]
    got += [send(pick(parts, (x + d) % 4, 1), "trans", along_x(d)) for d in (1, 2, 3)]
    own = choose((x - block // 4) % 4, got)
    swapped = tie(choose((x - other_block // 4) % 4, got), below, above)
    share = jnp.stack([own, send(swapped, "rows", CORE)], axis=1)
    share = (share.astype(F32) * coulomb).astype(BF16)
    share = share.reshape(4, 2, 4, 16, 512)
    got = [pick(share, (z + d) % 4, 2) for d in range(4)]
    *got, early_below, early_above = lax.optimization_barrier((*got, below, above))
    got[1:] = [send(got[d], "trans", along_z(d)) for d in (1, 2, 3)]
    low = send(early_below[:512], "gvec", along_y(1))
    high = send(early_above[512:], "gvec", along_y(3))
    share = choose((z - block % 4) % 4, got)
    got = [pick(share, y, 0)]
    got += [send(pick(share, (y + d) % 4, 0), "gvec", along_y(d)) for d in (1, 2, 3)]
    share = jnp.concatenate([piece[c] for c in range(2) for piece in got], axis=1)
    share, mine, twin, below, above, low, high = lax.optimization_barrier(
        (share, mine, twin, below, above, low, high)
    )
    below_twin = send(below, "rows", CORE)
    above_twin = send(above, "rows", CORE)
    low_twin = send(low, "rows", CORE)
    high_twin = send(high, "rows", CORE)
    first = [mine, below, None, above, twin, below_twin, None, above_twin]
    right = []
    for half, pair in enumerate(((low, low_twin), (high, high_twin))):
        parts = [v if v is None else v[512 * half : 512 * half + 512] for v in first]
        parts[2], parts[6] = pair
        right.append(jnp.concatenate(parts, axis=1))
    chunk = jnp.concatenate([share, *from_below(share, "trans", along_z)], axis=0)
    chunk, right = lax.optimization_barrier((chunk, right))
    one, three = send(chunk, "trans", along_x(1)), send(chunk, "trans", along_x(3))
    two = send(one[:32], "trans", along_x(1)), send(three[32:], "trans", along_x(3))
    others = (one, *two, three)
    sign = (1 - 2 * core).astype(BF16)

    def add(one, other):
        return (one.astype(F32) + other.astype(F32)).astype(BF16)

    own_terms = jnp.concatenate([multiply(chunk, sign, half) for half in right], axis=2)
    own_sum = add(own_terms, send(own_terms, "gvec", PAIR))
    own_sum, *others = lax.optimization_barrier((own_sum, *others))
    own_piece = gather(own_sum)
    others = jnp.concatenate(others)
    low_terms = multiply(others, sign, right[0])
    high_terms = multiply(tie(others, low_terms), sign, right[1])
    low_sum = add(low_terms, send(low_terms, "gvec", PAIR))
    low_sum = tie(low_sum, high_terms, own_piece[1], own_piece[3], *own_piece[2])
    low_piece = gather(low_sum)
    high_sum = add(high_terms, send(high_terms, "gvec", PAIR))
    high_piece = gather(high_sum)
    kernel_rows = own_rows(place, (own_sum, low_sum, high_sum))
    mirrored = None
    for half, piece in enumerate((low_piece, high_piece)):
        pieces = [value for d in range(4) for value in (own_piece[d], piece[d])]
        pieces[4:6] = [own_piece[2][0], piece[2][0], own_piece[2][1], piece[2][1]]
        mirrored = mirror(place, mirrored, half, pieces)
    return (kernel_rows, mirrored)


def solution(mesh):
    placed = (P(None, "trans", "gvec"), P("gvec"), P("rows"))
    return jax.shard_map(
        body,
        mesh=mesh,
        in_specs=placed,
        out_specs=(P(None, ("rows", "gvec"), "trans"), P(None, "trans", "rows")),
        check_vma=False,
    )
```

```python
import jax
import jax.numpy as jnp
from jax import lax
from jax.experimental import pallas as pl
from jax.experimental.pallas import tpu as pltpu
from jax.sharding import PartitionSpec as P

BF16 = jnp.bfloat16
F32 = jnp.float32
PAIR = [(2 * y + p, 2 * y + 1 - p) for y in range(4) for p in range(2)]
CORE = [(0, 1), (1, 0)]
LIMIT = 24 * 1024 * 1024


def along_x(step):
    return [(4 * x + z, 4 * ((x + step) % 4) + z) for x in range(4) for z in range(4)]


def along_z(step):
    return [(4 * x + z, 4 * x + (z + step) % 4) for x in range(4) for z in range(4)]


def along_y(step):
    return [(2 * y + p, 2 * ((y + step) % 4) + p) for y in range(4) for p in range(2)]


def send(value, axis, pairs):
    return lax.ppermute(value, axis, pairs)


def pick(value, index, axis):
    return lax.dynamic_index_in_dim(value, index, axis, keepdims=False)


def gather(value):
    one, three = send(value, "gvec", along_y(1)), send(value, "gvec", along_y(3))
    two = send(one[0], "gvec", along_y(1)), send(three[1], "gvec", along_y(3))
    return value, one, two, three


def choose(distance, candidates):
    out = candidates[0]
    for d in range(1, 4):
        out = jnp.where(distance == d, candidates[d], out)
    return out


def from_below(value, axis, pairs):
    one, three = send(value, axis, pairs(1)), send(value, axis, pairs(3))
    return one, send(value, axis, pairs(2)), three


def tie(value, *others):
    return lax.optimization_barrier((value, *others))[0]


def multiply(chunk, sign, right):
    rows, half = chunk.shape[0], chunk.shape[1] // 2
    turned = jnp.concatenate([-chunk[:, half:], chunk[:, :half]], axis=1) * sign
    left = jnp.concatenate([chunk, turned], axis=0)
    return contract(left, right).astype(BF16).reshape(2, rows, right.shape[0])


def contract(left, right):
    return lax.dot_general(
        left, right, (((1,), (1,)), ((), ())), preferred_element_type=F32
    )


def place_rows(ref, start, value, z, first=0):
    for k in range(4):
        to = pl.multiple_of(start + 16 * lax.rem(z + 4 - k, 4), 16)
        ref[pl.ds(to, 16), :] = value[first + 16 * k : first + 16 * k + 16, :]


def place_others(ref, value, x, z):
    for d in range(1, 4):
        place_rows(ref, 64 * lax.rem(x + 4 - d, 4), value, z, 64 * d - 64)


def mirror_kernel(place_ref, *refs):
    scratch, out_ref = refs[-1], refs[-2]
    y, x, z = place_ref[0], place_ref[1], place_ref[2]
    sign = jnp.where(pl.program_id(0) == 0, 1.0, -1.0).astype(BF16)
    groups = [refs[0:2], refs[2:4], None, refs[8:10]]
    for d in range(4):
        held = scratch.at[d]
        if d == 2:
            first = pl.program_id(0) == 0
            own = jnp.where(first, refs[4][...], refs[6][...])
            others = jnp.where(first, refs[5][...], refs[7][...])
        else:
            own, others = groups[d][0].at[0], groups[d][1].at[0]
        place_rows(held, 64 * x, own, z)
        place_others(held, others, x, z)
        columns = pl.ds(pl.multiple_of(256 * lax.rem(y + 4 - d, 4), 256), 256)
        out_ref[0, :, columns] = held[...].T * sign


def mirror(place, held, half, pieces):
    whole = [
        pl.BlockSpec((1, 64, 512), lambda c, s: (c, 0, half)),
        pl.BlockSpec((1, 192, 512), lambda c, s: (c, 0, 0)),
    ]
    single = [
        pl.BlockSpec((64, 512), lambda c, s: (0, half)),
        pl.BlockSpec((192, 512), lambda c, s: (0, 0)),
    ]
    specs = [*whole * 2, *single * 2, *whole]
    operands, aliases = list(pieces), {}
    if held is not None:
        specs.append(pl.BlockSpec(memory_space=pl.ANY))
        operands.append(held)
        aliases = {len(operands): 0}
    return pl.pallas_call(
        mirror_kernel,
        grid_spec=pltpu.PrefetchScalarGridSpec(
            num_scalar_prefetch=1,
            grid=(2,),
            in_specs=specs,
            out_specs=pl.BlockSpec((1, 512, 1024), lambda c, s: (c, half, 0)),
            scratch_shapes=[pltpu.VMEM((4, 256, 512), BF16)],
        ),
        out_shape=jax.ShapeDtypeStruct((2, 1024, 1024), BF16),
        input_output_aliases=aliases,
        compiler_params=pltpu.CompilerParams(vmem_limit_bytes=LIMIT),
        cost_estimate=pl.CostEstimate(flops=0, bytes_accessed=2**22, transcendentals=0),
    )(place, *operands)


def rows_kernel(place_ref, own, low, high, out_ref, scratch):
    x, z, p = place_ref[1], place_ref[2], place_ref[3]
    place_rows(scratch, 64 * x, own.at[0], z)
    for half, value in enumerate((low, high)):
        place_others(scratch.at[:, pl.ds(512 * half, 512)], value.at[0], x, z)
    out_ref[0] = scratch[pl.ds(pl.multiple_of(128 * p, 128), 128), :]


def own_rows(place, pieces):
    return pl.pallas_call(
        rows_kernel,
        grid_spec=pltpu.PrefetchScalarGridSpec(
            num_scalar_prefetch=1,
            grid=(2,),
            in_specs=[
                pl.BlockSpec((1, *piece.shape[1:]), lambda c, s: (c, 0, 0)) for piece in pieces
            ],
            out_specs=pl.BlockSpec((1, 128, 1024), lambda c, s: (c, 0, 0)),
            scratch_shapes=[pltpu.VMEM((256, 1024), BF16)],
        ),
        out_shape=jax.ShapeDtypeStruct((2, 128, 1024), BF16),
        compiler_params=pltpu.CompilerParams(vmem_limit_bytes=LIMIT),
        cost_estimate=pl.CostEstimate(flops=0, bytes_accessed=3 * 2**19, transcendentals=0),
    )(place, *pieces)


def body(pair_density, coulomb, block_index):
    core = lax.axis_index("rows")
    trans = lax.axis_index("trans")
    gvec = lax.axis_index("gvec")
    x, z = trans // 4, trans % 4
    y, p = gvec // 2, gvec % 2
    place = jnp.stack([y, x, z, p]).astype(jnp.int32)
    block = block_index[0]
    other_block = send(block_index, "rows", CORE)[0]

    mine = pick(pair_density, core, 0)
    twin = pick(pair_density, 1 - core, 0)
    below = send(mine, "gvec", along_y(1))
    above = send(mine, "gvec", along_y(3))

    parts = mine.reshape(4, 4, 64, 512)
    got = [pick(parts, x, 1)]
    got += [send(pick(parts, (x + d) % 4, 1), "trans", along_x(d)) for d in (1, 2, 3)]
    swapped = choose((x - other_block // 4) % 4, got)
    *got, swapped = lax.optimization_barrier((*got, swapped))
    swapped = tie(send(swapped, "rows", CORE), below, above)
    share = jnp.stack([choose((x - block // 4) % 4, got), swapped], axis=1)
    share = (share.astype(F32) * coulomb).astype(BF16)
    share = share.reshape(4, 2, 4, 16, 512)
    got = [pick(share, (z + d) % 4, 2) for d in range(4)]
    *got, early_below, early_above = lax.optimization_barrier((*got, below, above))
    got[1:] = [send(got[d], "trans", along_z(d)) for d in (1, 2, 3)]
    low = send(early_below[:512], "gvec", along_y(1))
    high = send(early_above[512:], "gvec", along_y(3))
    share = choose((z - block % 4) % 4, got)
    got = [pick(share, y, 0)]
    got += [send(pick(share, (y + d) % 4, 0), "gvec", along_y(d)) for d in (1, 2, 3)]
    share = jnp.concatenate([piece[c] for c in range(2) for piece in got], axis=1)
    share, mine, twin, below, above, low, high = lax.optimization_barrier(
        (share, mine, twin, below, above, low, high)
    )
    below_twin = send(below, "rows", CORE)
    above_twin = send(above, "rows", CORE)
    low_twin = send(low, "rows", CORE)
    high_twin = send(high, "rows", CORE)
    first = [mine, below, None, above, twin, below_twin, None, above_twin]
    right = []
    for half, pair in enumerate(((low, low_twin), (high, high_twin))):
        parts = [v if v is None else v[512 * half : 512 * half + 512] for v in first]
        parts[2], parts[6] = pair
        right.append(jnp.concatenate(parts, axis=1))
    chunk = jnp.concatenate([share, *from_below(share, "trans", along_z)], axis=0)
    chunk, right = lax.optimization_barrier((chunk, right))
    one, three = send(chunk, "trans", along_x(1)), send(chunk, "trans", along_x(3))
    two = send(one[:32], "trans", along_x(1)), send(three[32:], "trans", along_x(3))
    sign = (1 - 2 * core).astype(BF16)

    def add(one, other):
        return (one.astype(F32) + other.astype(F32)).astype(BF16)

    own_terms = jnp.concatenate([multiply(chunk, sign, half) for half in right], axis=2)
    own_sum = add(own_terms, send(own_terms, "gvec", PAIR))
    own_sum, one, three = lax.optimization_barrier((own_sum, one, three))
    own_piece = gather(own_sum)
    others = jnp.concatenate([one, *two, three])
    low_terms = multiply(others, sign, right[0])
    high_terms = multiply(tie(others, low_terms), sign, right[1])
    low_sum = add(low_terms, send(low_terms, "gvec", PAIR))
    low_sum = tie(low_sum, high_terms, own_piece[1], own_piece[3], *own_piece[2])
    low_piece = gather(low_sum)
    high_sum = add(high_terms, send(high_terms, "gvec", PAIR))
    high_piece = gather(high_sum)
    kernel_rows = own_rows(place, (own_sum, low_sum, high_sum))
    mirrored = None
    for half, piece in enumerate((low_piece, high_piece)):
        pieces = [value for d in range(4) for value in (own_piece[d], piece[d])]
        pieces[4:6] = [own_piece[2][0], piece[2][0], own_piece[2][1], piece[2][1]]
        mirrored = mirror(place, mirrored, half, pieces)
    return (kernel_rows, mirrored)


def solution(mesh):
    placed = (P(None, "trans", "gvec"), P("gvec"), P("rows"))
    return jax.shard_map(
        body,
        mesh=mesh,
        in_specs=placed,
        out_specs=(P(None, ("rows", "gvec"), "trans"), P(None, "trans", "rows")),
        check_vma=False,
    )
```

```python
import jax
import jax.numpy as jnp
from jax import lax
from jax.experimental import pallas as pl
from jax.experimental.pallas import tpu as pltpu
from jax.sharding import PartitionSpec as P

BF16 = jnp.bfloat16
F32 = jnp.float32
PAIR = [(2 * y + p, 2 * y + 1 - p) for y in range(4) for p in range(2)]
CORE = [(0, 1), (1, 0)]
LIMIT = 24 * 1024 * 1024


def along_x(step):
    return [(4 * x + z, 4 * ((x + step) % 4) + z) for x in range(4) for z in range(4)]


def along_z(step):
    return [(4 * x + z, 4 * x + (z + step) % 4) for x in range(4) for z in range(4)]


def along_y(step):
    return [(2 * y + p, 2 * ((y + step) % 4) + p) for y in range(4) for p in range(2)]


def send(value, axis, pairs):
    return lax.ppermute(value, axis, pairs)


def pick(value, index, axis):
    return lax.dynamic_index_in_dim(value, index, axis, keepdims=False)


def gather(value, *others):
    one, three = send(value, "gvec", along_y(1)), send(value, "gvec", along_y(3))
    one, three, *_ = lax.optimization_barrier((one, three, *others))
    two = send(one[0], "gvec", along_y(1)), send(three[1], "gvec", along_y(3))
    return value, one, two, three


def choose(distance, candidates):
    out = candidates[0]
    for d in range(1, 4):
        out = jnp.where(distance == d, candidates[d], out)
    return out


def from_below(value, axis, pairs):
    one, three = send(value, axis, pairs(1)), send(value, axis, pairs(3))
    return one, send(value, axis, pairs(2)), three


def tie(value, *others):
    return lax.optimization_barrier((value, *others))[0]


def multiply(chunk, sign, right):
    rows, half = chunk.shape[0], chunk.shape[1] // 2
    turned = jnp.concatenate([-chunk[:, half:], chunk[:, :half]], axis=1) * sign
    left = jnp.concatenate([chunk, turned], axis=0)
    return contract(left, right).astype(BF16).reshape(2, rows, right.shape[0])


def contract(left, right):
    return lax.dot_general(
        left, right, (((1,), (1,)), ((), ())), preferred_element_type=F32
    )


def place_rows(ref, start, value, z, first=0):
    for k in range(4):
        to = pl.multiple_of(start + 16 * lax.rem(z + 4 - k, 4), 16)
        ref[pl.ds(to, 16), :] = value[first + 16 * k : first + 16 * k + 16, :]


def place_others(ref, value, x, z):
    for d in range(1, 4):
        place_rows(ref, 64 * lax.rem(x + 4 - d, 4), value, z, 64 * d - 64)


def mirror_kernel(place_ref, *refs):
    scratch, out_ref = refs[-1], refs[-2]
    y, x, z = place_ref[0], place_ref[1], place_ref[2]
    sign = jnp.where(pl.program_id(0) == 0, 1.0, -1.0).astype(BF16)
    groups = [refs[0:2], refs[2:4], None, refs[8:10]]
    for d in range(4):
        held = scratch.at[d]
        if d == 2:
            first = pl.program_id(0) == 0
            own = jnp.where(first, refs[4][...], refs[6][...])
            others = jnp.where(first, refs[5][...], refs[7][...])
        else:
            own, others = groups[d][0].at[0], groups[d][1].at[0]
        place_rows(held, 64 * x, own, z)
        place_others(held, others, x, z)
        columns = pl.ds(pl.multiple_of(256 * lax.rem(y + 4 - d, 4), 256), 256)
        out_ref[0, :, columns] = held[...].T * sign


def mirror(place, held, half, pieces):
    whole = [
        pl.BlockSpec((1, 64, 512), lambda c, s: (c, 0, half)),
        pl.BlockSpec((1, 192, 512), lambda c, s: (c, 0, 0)),
    ]
    single = [
        pl.BlockSpec((64, 512), lambda c, s: (0, half)),
        pl.BlockSpec((192, 512), lambda c, s: (0, 0)),
    ]
    specs = [*whole * 2, *single * 2, *whole]
    operands, aliases = list(pieces), {}
    if held is not None:
        specs.append(pl.BlockSpec(memory_space=pl.ANY))
        operands.append(held)
        aliases = {len(operands): 0}
    return pl.pallas_call(
        mirror_kernel,
        grid_spec=pltpu.PrefetchScalarGridSpec(
            num_scalar_prefetch=1,
            grid=(2,),
            in_specs=specs,
            out_specs=pl.BlockSpec((1, 512, 1024), lambda c, s: (c, half, 0)),
            scratch_shapes=[pltpu.VMEM((4, 256, 512), BF16)],
        ),
        out_shape=jax.ShapeDtypeStruct((2, 1024, 1024), BF16),
        input_output_aliases=aliases,
        compiler_params=pltpu.CompilerParams(vmem_limit_bytes=LIMIT),
        cost_estimate=pl.CostEstimate(flops=0, bytes_accessed=2**22, transcendentals=0),
    )(place, *operands)


def rows_kernel(place_ref, own, low, high, out_ref, scratch):
    x, z, p = place_ref[1], place_ref[2], place_ref[3]
    place_rows(scratch, 64 * x, own.at[0], z)
    for half, value in enumerate((low, high)):
        place_others(scratch.at[:, pl.ds(512 * half, 512)], value.at[0], x, z)
    out_ref[0] = scratch[pl.ds(pl.multiple_of(128 * p, 128), 128), :]


def own_rows(place, pieces):
    return pl.pallas_call(
        rows_kernel,
        grid_spec=pltpu.PrefetchScalarGridSpec(
            num_scalar_prefetch=1,
            grid=(2,),
            in_specs=[
                pl.BlockSpec((1, *piece.shape[1:]), lambda c, s: (c, 0, 0)) for piece in pieces
            ],
            out_specs=pl.BlockSpec((1, 128, 1024), lambda c, s: (c, 0, 0)),
            scratch_shapes=[pltpu.VMEM((256, 1024), BF16)],
        ),
        out_shape=jax.ShapeDtypeStruct((2, 128, 1024), BF16),
        compiler_params=pltpu.CompilerParams(vmem_limit_bytes=LIMIT),
        cost_estimate=pl.CostEstimate(flops=0, bytes_accessed=3 * 2**19, transcendentals=0),
    )(place, *pieces)


def body(pair_density, coulomb, block_index):
    core = lax.axis_index("rows")
    trans = lax.axis_index("trans")
    gvec = lax.axis_index("gvec")
    x, z = trans // 4, trans % 4
    y, p = gvec // 2, gvec % 2
    place = jnp.stack([y, x, z, p]).astype(jnp.int32)
    block = block_index[0]
    other_block = send(block_index, "rows", CORE)[0]

    mine = pick(pair_density, core, 0)
    twin = pick(pair_density, 1 - core, 0)
    below = send(mine, "gvec", along_y(1))
    above = send(mine, "gvec", along_y(3))

    parts = mine.reshape(4, 4, 64, 512)
    got = [pick(parts, x, 1)]
    got += [send(pick(parts, (x + d) % 4, 1), "trans", along_x(d)) for d in (1, 2, 3)]
    swapped = choose((x - other_block // 4) % 4, got)
    *got, swapped = lax.optimization_barrier((*got, swapped))
    swapped = tie(send(swapped, "rows", CORE), below, above)
    share = jnp.stack([choose((x - block // 4) % 4, got), swapped], axis=1)
    share = (share.astype(F32) * coulomb).astype(BF16)
    share = share.reshape(4, 2, 4, 16, 512)
    got = [pick(share, (z + d) % 4, 2) for d in range(4)]
    *got, early_below, early_above = lax.optimization_barrier((*got, below, above))
    got[1:] = [send(got[d], "trans", along_z(d)) for d in (1, 2, 3)]
    low = send(early_below[:512], "gvec", along_y(1))
    high = send(early_above[512:], "gvec", along_y(3))
    share = choose((z - block % 4) % 4, got)
    got = [pick(share, y, 0)]
    got += [send(pick(share, (y + d) % 4, 0), "gvec", along_y(d)) for d in (1, 2, 3)]
    share = jnp.concatenate([piece[c] for c in range(2) for piece in got], axis=1)
    share, mine, twin, below, above, low, high = lax.optimization_barrier(
        (share, mine, twin, below, above, low, high)
    )
    below_twin = send(below, "rows", CORE)
    above_twin = send(above, "rows", CORE)
    low_twin = send(low, "rows", CORE)
    high_twin = send(high, "rows", CORE)
    first = [mine, below, None, above, twin, below_twin, None, above_twin]
    right = []
    for half, pair in enumerate(((low, low_twin), (high, high_twin))):
        parts = [v if v is None else v[512 * half : 512 * half + 512] for v in first]
        parts[2], parts[6] = pair
        right.append(jnp.concatenate(parts, axis=1))
    chunk = jnp.concatenate([share, *from_below(share, "trans", along_z)], axis=0)
    chunk, right = lax.optimization_barrier((chunk, right))
    one, three = send(chunk, "trans", along_x(1)), send(chunk, "trans", along_x(3))
    two = send(one[:32], "trans", along_x(1)), send(three[32:], "trans", along_x(3))
    sign = (1 - 2 * core).astype(BF16)

    def add(one, other):
        return (one.astype(F32) + other.astype(F32)).astype(BF16)

    own_terms = jnp.concatenate([multiply(chunk, sign, half) for half in right], axis=2)
    own_sum = add(own_terms, send(own_terms, "gvec", PAIR))
    own_sum, one, three = lax.optimization_barrier((own_sum, one, three))
    own_piece = gather(own_sum)
    others = jnp.concatenate([one, *two, three])
    low_terms = multiply(others, sign, right[0])
    high_terms = multiply(tie(others, low_terms), sign, right[1])
    low_sum = add(low_terms, send(low_terms, "gvec", PAIR))
    low_sum = tie(low_sum, high_terms, own_piece[1], own_piece[3], *own_piece[2])
    low_piece = gather(low_sum)
    high_sum = add(high_terms, send(high_terms, "gvec", PAIR))
    kernel_rows = own_rows(place, (own_sum, low_sum, high_sum))
    high_piece = gather(high_sum, kernel_rows)
    mirrored = None
    for half, piece in enumerate((low_piece, high_piece)):
        pieces = [value for d in range(4) for value in (own_piece[d], piece[d])]
        pieces[4:6] = [own_piece[2][0], piece[2][0], own_piece[2][1], piece[2][1]]
        mirrored = mirror(place, mirrored, half, pieces)
    return (kernel_rows, mirrored)


def solution(mesh):
    placed = (P(None, "trans", "gvec"), P("gvec"), P("rows"))
    return jax.shard_map(
        body,
        mesh=mesh,
        in_specs=placed,
        out_specs=(P(None, ("rows", "gvec"), "trans"), P(None, "trans", "rows")),
        check_vma=False,
    )
```
